32 devices in a mesh: row: 4 (over y, x), col: 4 (over z), depth: 2 (over core).
Axes of the slice: x: 2, y: 2, z: 4, core: 2. Of those that a mesh axis runs over, the one named last changes fastest.
Arguments:
- tokens: bfloat16 [128, 8192], P(('row', 'depth'), 'col'), may hold values from -6 to 6
- cotangent: bfloat16 [128, 8192], P(('row', 'depth'), 'col'), may hold values from -6 to 6
- gate_weight: bfloat16 [8192, 14336], P('col', ('row', 'depth')), may hold values from -0.0625 to 0.0625
- up_weight: bfloat16 [8192, 14336], P('col', ('row', 'depth')), may hold values from -0.0625 to 0.0625
- down_weight: bfloat16 [14336, 8192], P(('row', 'depth'), 'col'), may hold values from -0.046875 to 0.046875
Outputs:
- layer_out: bfloat16 [128, 8192], P(('row', 'depth'), 'col')
- tokens_grad: bfloat16 [128, 8192], P(('row', 'depth'), 'col')
- gate_grad: bfloat16 [8192, 14336], P('col', ('row', 'depth'))
- up_grad: bfloat16 [8192, 14336], P('col', ('row', 'depth'))
- down_grad: bfloat16 [14336, 8192], P(('row', 'depth'), 'col')
The draws below stay inside these ranges and needn't reach their ends.
All inputs are finite; a program needn't handle non-finite values.
Results may differ from the reference program's by a relative error of at most 0.0049.
Values may be sent and summed in bfloat16 or wider, within the bound.
A program may use at most 128 MiB of HBM per device.

```python
import math
import jax
import jax.numpy as jnp

D = 8192
FF = 14336
TOKENS = 128


def block_levels(rng, shape, cuts, smallest, largest):
    factor_of = 1.0
    for axis_at, blocks in cuts:
        draws = jax.random.uniform(jax.random.fold_in(jax.random.fold_in(rng, 6), axis_at), (blocks,), jnp.float32, smallest / len(cuts), largest / len(cuts))
        factor_of = factor_of * jnp.repeat(jnp.exp(draws), shape[axis_at] // blocks).reshape((-1,) + (1,) * (len(shape) - 1 - axis_at))
    return factor_of


def bell_draw(key, shape, spread, reach, split=(), held_as=jnp.bfloat16):
    gain = block_levels(key, shape, split, -0.22, 0.18) if split else 1.0
    values = jax.random.normal(key, shape, jnp.float32) * spread * gain
    return jnp.minimum(jnp.maximum(values, -reach), reach).astype(held_as)


def setup_inputs(seed: int = 0) -> dict:
    key_list = jax.random.split(jax.random.key(seed), 6)
    tokens = bell_draw(key_list[0], (TOKENS, D), 1.0, 6.0, ((0, 8), (1, 4)))
    cotangent = bell_draw(key_list[1], (TOKENS, D), 1.0, 6.0, ((0, 8), (1, 4)))
    gate_weight = bell_draw(key_list[2], (D, FF), D ** -0.5, 0.0625, ((0, 4), (1, 8)))
    up_weight = bell_draw(key_list[3], (D, FF), D ** -0.5, 0.0625, ((0, 4), (1, 8)))
    down_weight = bell_draw(key_list[4], (FF, D), FF ** -0.5, 0.046875, ((0, 8), (1, 4)))
    return {"tokens": tokens, "cotangent": cotangent, "gate_weight": gate_weight, "up_weight": up_weight, "down_weight": down_weight}


def reference(tokens, cotangent, gate_weight, up_weight, down_weight):
    gate_sum = jnp.dot(tokens, gate_weight, preferred_element_type=jnp.float32)
    up_sum = jnp.dot(tokens, up_weight, preferred_element_type=jnp.float32)
    sigmoid_gate = jax.nn.sigmoid(gate_sum)
    hidden = (gate_sum * sigmoid_gate * up_sum).astype(jnp.bfloat16)
    layer_out = jnp.dot(hidden, down_weight, preferred_element_type=jnp.float32).astype(jnp.bfloat16)
    hidden_cot = jnp.dot(cotangent, down_weight.T, preferred_element_type=jnp.float32)
    grad_scale = 1.0 / math.sqrt(TOKENS)
    down_grad = (jnp.dot(hidden.T, cotangent, preferred_element_type=jnp.float32) * grad_scale).astype(jnp.bfloat16)
    gate_cot = (hidden_cot * up_sum * sigmoid_gate * (1.0 + gate_sum * (1.0 - sigmoid_gate))).astype(jnp.bfloat16)
    up_cot = (hidden_cot * gate_sum * sigmoid_gate).astype(jnp.bfloat16)
    gate_grad = (jnp.dot(tokens.T, gate_cot, preferred_element_type=jnp.float32) * grad_scale).astype(jnp.bfloat16)
    up_grad = (jnp.dot(tokens.T, up_cot, preferred_element_type=jnp.float32) * grad_scale).astype(jnp.bfloat16)
    back_sum = jnp.dot(gate_cot, gate_weight.T, preferred_element_type=jnp.float32)
    back_sum = back_sum + jnp.dot(up_cot, up_weight.T, preferred_element_type=jnp.float32)
    tokens_grad = back_sum.astype(jnp.bfloat16)
    return (layer_out, tokens_grad, gate_grad, up_grad, down_grad)
```

```python
import functools
import math

import jax
import jax.numpy as jnp
from jax import lax
from jax.experimental import pallas as pl
from jax.experimental.pallas import tpu as pltpu
from jax.sharding import PartitionSpec as P

F32 = jnp.float32
BF16 = jnp.bfloat16
MESH = pl.DeviceIdType.MESH
VMEM_BYTES = 58 * 1024 * 1024
AG_SKEW = 3


def dot_nn(left, right):
    return lax.dot_general(left, right, (((1,), (0,)), ((), ())), preferred_element_type=F32)


def dot_nt(left, right):
    return lax.dot_general(left, right, (((1,), (1,)), ((), ())), preferred_element_type=F32)


def dot_tn(left, right):
    return lax.dot_general(left, right, (((0,), (0,)), ((), ())), preferred_element_type=F32)


def layer_kernel(
    rows, cols, depths,
    tok, cot, gw, uw, dw,
    out, tgrad, tok_all, cot_all, res,
    gwv, uwv, dwv, part, sbuf, rbuf, acc, abuf, bsend, brecv, own,
    wsem, g1_send, g1_recv, g2_send, g2_recv,
    rs_send, rs_recv, ag_send, ag_recv,
    a_send, a_recv, b_send, b_recv,
):
    chunks, _, width = gwv.shape
    block = tok.shape[0]
    total = tok_all.shape[0]
    half = total // 2
    wire = sbuf.dtype
    r = lax.axis_index("row")
    z = lax.axis_index("col")
    d = lax.axis_index("depth")

    def rows_of(index):
        return pl.ds(pl.multiple_of(index * block, block), block)

    def weight_copies(c):
        span = slice(None) if chunks == 1 else pl.ds(pl.multiple_of(c * width, width), width)
        return (
            pltpu.make_async_copy(gw.at[:, span], gwv.at[c], wsem.at[0, c]),
            pltpu.make_async_copy(uw.at[:, span], uwv.at[c], wsem.at[1, c]),
            pltpu.make_async_copy(dw.at[span, :], dwv.at[c], wsem.at[2, c]),
        )

    for c in range(chunks):
        for copy in weight_copies(c):
            copy.start()

    barrier = pltpu.get_barrier_semaphore()
    for k in range(1, rows):
        pl.semaphore_signal(barrier, inc=1, device_id={"row": lax.rem(r + k, rows)}, device_id_type=MESH)
    for j in range(1, depths):
        pl.semaphore_signal(barrier, inc=1, device_id={"depth": lax.rem(d + j, depths)}, device_id_type=MESH)

    @pl.when(z > 0)
    def _():
        pl.semaphore_signal(barrier, inc=1, device_id={"col": z - 1}, device_id_type=MESH)

    @pl.when(z < cols - 1)
    def _():
        pl.semaphore_signal(barrier, inc=1, device_id={"col": z + 1}, device_id_type=MESH)

    for a, (mine, everyone) in enumerate(((tok, tok_all), (cot, cot_all))):
        everyone[rows_of(r * depths + d), :] = mine[...]
    acc[...] = jnp.zeros_like(acc)

    near = (rows - 1) + (depths - 1)

    @pl.when(jnp.logical_or(z == 0, z == cols - 1))
    def _():
        pl.semaphore_wait(barrier, near + 1)

    @pl.when(jnp.logical_and(z > 0, z < cols - 1))
    def _():
        pl.semaphore_wait(barrier, near + 2)

    pairs = ((tok, tok_all), (cot, cot_all))

    def first_hop(a, k, source_row):
        mine, everyone = pairs[a]
        return pltpu.make_async_remote_copy(
            src_ref=mine,
            dst_ref=everyone.at[rows_of(source_row * depths + d), :],
            send_sem=g1_send.at[a, k - 1],
            recv_sem=g1_recv.at[a, k - 1],
            device_id={"row": lax.rem(r + k, rows)},
            device_id_type=MESH,
        )

    def second_hop(a, k, j, source_depth):
        everyone = pairs[a][1]
        where = rows_of(lax.rem(r - k + rows, rows) * depths + source_depth)
        return pltpu.make_async_remote_copy(
            src_ref=everyone.at[where, :],
            dst_ref=everyone.at[where, :],
            send_sem=g2_send.at[a, k, j - 1],
            recv_sem=g2_recv.at[a, k, j - 1],
            device_id={"depth": lax.rem(d + j, depths)},
            device_id_type=MESH,
        )

    for k in range(1, rows):
        for a in range(2):
            first_hop(a, k, r).start()
    for k in range(rows):
        for a in range(2):
            if k:
                first_hop(a, k, lax.rem(r - k + rows, rows)).wait_recv()
            for j in range(1, depths):
                second_hop(a, k, j, d).start()
    for k in range(rows):
        for a in range(2):
            for j in range(1, depths):
                second_hop(a, k, j, lax.rem(d - j + depths, depths)).wait_recv()

    def position(way):
        return z if way == 0 else cols - 1 - z

    def token_rows(way):
        return pl.ds(half, half) if way == 0 else pl.ds(0, half)

    def sum_copy(way, c):
        target = lax.rem(z + 1, cols) if way == 0 else lax.rem(z + cols - 1, cols)
        return pltpu.make_async_remote_copy(
            src_ref=sbuf.at[way, c],
            dst_ref=rbuf.at[way, c],
            send_sem=rs_send.at[way, c],
            recv_sem=rs_recv.at[way, c],
            device_id={"col": target},
            device_id_type=MESH,
        )

    def result_copy(way, c):
        target = lax.rem(z + cols - 1, cols) if way == 0 else lax.rem(z + 1, cols)
        where = res.at[c, :, token_rows(way), :]
        return pltpu.make_async_remote_copy(
            src_ref=where,
            dst_ref=where,
            send_sem=ag_send.at[way, c],
            recv_sem=ag_recv.at[way, c],
            device_id={"col": target},
            device_id_type=MESH,
        )

    def partial_sums(c):
        for copy in weight_copies(c):
            copy.wait()
        part[c, 0] = dot_nn(tok_all[...], gwv[c])
        part[c, 1] = dot_nn(tok_all[...], uwv[c])
        part[c, 2] = dot_nt(cot_all[...], dwv[c])

    def pass_sum(way, c):
        at = position(way)
        mine = token_rows(way)

        @pl.when(at == 0)
        def _():
            sbuf[way, c] = part[c, :, mine, :].astype(wire)
            sum_copy(way, c).start()

        @pl.when(jnp.logical_and(at > 0, at < cols - 1))
        def _():
            sum_copy(way, c).wait_recv()
            sbuf[way, c] = (part[c, :, mine, :] + rbuf[way, c].astype(F32)).astype(wire)
            sum_copy(way, c).start()

        @pl.when(at == cols - 1)
        def _():
            sum_copy(way, c).wait_recv()
            gate = part[c, 0, mine, :] + rbuf[way, c, 0].astype(F32)
            up = part[c, 1, mine, :] + rbuf[way, c, 1].astype(F32)
            hidden_cot = part[c, 2, mine, :] + rbuf[way, c, 2].astype(F32)
            sig = jax.nn.sigmoid(gate)
            res[c, 0, mine, :] = (gate * sig * up).astype(BF16)
            res[c, 1, mine, :] = (hidden_cot * up * sig * (1.0 + gate * (1.0 - sig))).astype(BF16)
            res[c, 2, mine, :] = (hidden_cot * gate * sig).astype(BF16)
            result_copy(way, c).start()

    def pass_result(way, c):
        at = position(way)

        @pl.when(at < cols - 1)
        def _():
            result_copy(way, c).wait_recv()

        @pl.when(jnp.logical_and(at > 0, at < cols - 1))
        def _():
            result_copy(way, c).start()

    def add_outputs(c):
        acc[0] += dot_nn(res[c, 0], dwv[c])
        acc[1] += dot_nt(res[c, 1], gwv[c]) + dot_nt(res[c, 2], uwv[c])

    def step(s, carry):
        @pl.when(s < chunks)
        def _():
            partial_sums(s)

        @pl.when(jnp.logical_and(s >= 1, s < chunks + 1))
        def _():
            pass_sum(0, s - 1)
            pass_sum(1, s - 1)

        @pl.when(s >= 1 + AG_SKEW)
        def _():
            c = s - 1 - AG_SKEW
            pass_result(0, c)
            pass_result(1, c)
            add_outputs(c)

        return carry

    lax.fori_loop(0, chunks + 1 + AG_SKEW, step, 0)

    def depth_copy(a, row, j, target_depth):
        return pltpu.make_async_remote_copy(
            src_ref=acc.at[a, pl.ds(pl.multiple_of((row * depths + target_depth) * block, block), block), :],
            dst_ref=abuf.at[j - 1, row, a],
            send_sem=a_send.at[j - 1, row, a],
            recv_sem=a_recv.at[j - 1, row, a],
            device_id={"depth": lax.rem(d + j, depths)},
            device_id_type=MESH,
        )

    def row_copy(k):
        return pltpu.make_async_remote_copy(
            src_ref=bsend.at[k - 1],
            dst_ref=brecv.at[k - 1],
            send_sem=b_send.at[k - 1],
            recv_sem=b_recv.at[k - 1],
            device_id={"row": lax.rem(r + k, rows)},
            device_id_type=MESH,
        )

    for row in range(rows):
        for a in range(2):
            for j in range(1, depths):
                depth_copy(a, row, j, lax.rem(d + j, depths)).start()
    for row in range(rows):
        for a in range(2):
            for j in range(1, depths):
                depth_copy(a, row, j, lax.rem(d + j, depths)).wait_recv()
    for k in list(range(1, rows)) + [0]:
        row = lax.rem(r + k, rows)
        for a in range(2):
            value = acc[a, rows_of(row * depths + d), :]
            for j in range(1, depths):
                value = value + abuf[j - 1, row, a]
            if k:
                bsend[k - 1, a] = value.astype(wire)
            else:
                own[a] = value
        if k:
            row_copy(k).start()
    for k in range(1, rows):
        row_copy(k).wait_recv()
    for a, result in enumerate((out, tgrad)):
        value = own[a]
        for k in range(1, rows):
            value = value + brecv[k - 1, a].astype(F32)
        result[...] = value.astype(result.dtype)

    for k in range(1, rows):
        row_copy(k).wait_send()
        for a in range(2):
            first_hop(a, k, r).wait_send()
    for a in range(2):
        for k in range(rows):
            for j in range(1, depths):
                second_hop(a, k, j, d).wait_send()
                depth_copy(a, k, j, lax.rem(d + j, depths)).wait_send()

    def drain(c, carry):
        for way in range(2):
            at = position(way)

            @pl.when(at < cols - 1)
            def _():
                sum_copy(way, c).wait_send()

            @pl.when(at > 0)
            def _():
                result_copy(way, c).wait_send()

        return carry

    lax.fori_loop(0, chunks, drain, 0)


def grads_kernel(scale, tok_all, cot_all, res, gate_grad, up_grad, down_grad):
    gate_grad[...] = (dot_tn(tok_all[...], res[0, 1]) * scale).astype(BF16)
    up_grad[...] = (dot_tn(tok_all[...], res[0, 2]) * scale).astype(BF16)
    down_grad[...] = (dot_tn(res[0, 0], cot_all[...]) * scale).astype(BF16)


def shards(rows, cols, depths, tokens, cotangent, gate_weight, up_weight, down_weight):
    block, feats = tokens.shape
    units = gate_weight.shape[1]
    total = block * rows * depths
    half = total // 2
    width = 256 if units % 256 == 0 else units
    chunks = units // width
    wire = BF16 if cols <= 4 else F32
    vmem = pl.BlockSpec(memory_space=pltpu.VMEM)
    hbm = pl.BlockSpec(memory_space=pl.ANY)
    dma = pltpu.SemaphoreType.DMA
    out, tgrad, tok_all, cot_all, res = pl.pallas_call(
        functools.partial(layer_kernel, rows, cols, depths),
        out_shape=(
            jax.ShapeDtypeStruct((block, feats), BF16),
            jax.ShapeDtypeStruct((block, feats), BF16),
            jax.ShapeDtypeStruct((total, feats), BF16),
            jax.ShapeDtypeStruct((total, feats), BF16),
            jax.ShapeDtypeStruct((chunks, 3, total, width), BF16),
        ),
        in_specs=[vmem, vmem, hbm, hbm, hbm],
        out_specs=(vmem,) * 5,
        scratch_shapes=[
            pltpu.VMEM((chunks, feats, width), BF16),
            pltpu.VMEM((chunks, feats, width), BF16),
            pltpu.VMEM((chunks, width, feats), BF16),
            pltpu.VMEM((chunks, 3, total, width), F32),
            pltpu.VMEM((2, chunks, 3, half, width), wire),
            pltpu.VMEM((2, chunks, 3, half, width), wire),
            pltpu.VMEM((2, total, feats), F32),
            pltpu.VMEM((depths - 1, rows, 2, block, feats), F32),
            pltpu.VMEM((rows - 1, 2, block, feats), wire),
            pltpu.VMEM((rows - 1, 2, block, feats), wire),
            pltpu.VMEM((2, block, feats), F32),
            dma((3, chunks)),
            dma((2, rows - 1)),
            dma((2, rows - 1)),
            dma((2, rows, depths - 1)),
            dma((2, rows, depths - 1)),
            dma((2, chunks)),
            dma((2, chunks)),
            dma((2, chunks)),
            dma((2, chunks)),
            dma((depths - 1, rows, 2)),
            dma((depths - 1, rows, 2)),
            dma((rows - 1,)),
            dma((rows - 1,)),
        ],
        compiler_params=pltpu.CompilerParams(
            collective_id=0, has_side_effects=True, vmem_limit_bytes=VMEM_BYTES
        ),
    )(tokens, cotangent, gate_weight, up_weight, down_weight)

    whole = pl.BlockSpec((total, feats), lambda c: (0, 0))
    gate_grad, up_grad, down_grad = pl.pallas_call(
        functools.partial(grads_kernel, 1.0 / math.sqrt(total)),
        out_shape=(
            jax.ShapeDtypeStruct((feats, units), BF16),
            jax.ShapeDtypeStruct((feats, units), BF16),
            jax.ShapeDtypeStruct((units, feats), BF16),
        ),
        grid=(chunks,),
        in_specs=[whole, whole, pl.BlockSpec((1, 3, total, width), lambda c: (c, 0, 0, 0))],
        out_specs=(
            pl.BlockSpec((feats, width), lambda c: (0, c)),
            pl.BlockSpec((feats, width), lambda c: (0, c)),
            pl.BlockSpec((width, feats), lambda c: (c, 0)),
        ),
        compiler_params=pltpu.CompilerParams(vmem_limit_bytes=VMEM_BYTES),
    )(tok_all, cot_all, res)
    return (out, tgrad, gate_grad, up_grad, down_grad)


def solution(mesh):
    specs = (
        P(("row", "depth"), "col"),
        P(("row", "depth"), "col"),
        P("col", ("row", "depth")),
        P("col", ("row", "depth")),
        P(("row", "depth"), "col"),
    )
    sizes = (mesh.shape["row"], mesh.shape["col"], mesh.shape["depth"])
    return jax.shard_map(
        functools.partial(shards, *sizes), mesh=mesh, in_specs=specs, out_specs=specs, check_vma=False
    )
```

```python
import functools
import math

import jax
import jax.numpy as jnp
from jax import lax
from jax.experimental import pallas as pl
from jax.experimental.pallas import tpu as pltpu
from jax.sharding import PartitionSpec as P

F32 = jnp.float32
BF16 = jnp.bfloat16
MESH = pl.DeviceIdType.MESH
VMEM_BYTES = 58 * 1024 * 1024


def dot_nn(left, right):
    return lax.dot_general(left, right, (((1,), (0,)), ((), ())), preferred_element_type=F32)


def dot_nt(left, right):
    return lax.dot_general(left, right, (((1,), (1,)), ((), ())), preferred_element_type=F32)


def dot_tn(left, right):
    return lax.dot_general(left, right, (((0,), (0,)), ((), ())), preferred_element_type=F32)


def layer_kernel(
    rows, cols, depths,
    tok, cot, gw, uw, dw,
    sums, tok_all, cot_all, res,
    gwv, uwv, dwv, part, sbuf, rbuf, acc, abuf, bsend, brecv, own,
    wsem, g1_send, g1_recv, g2_send, g2_recv,
    rs_send, rs_recv, ag_send, ag_recv,
    a_send, a_recv, b_send, b_recv,
):
    chunks, _, width = gwv.shape
    block = tok.shape[0]
    total = tok_all.shape[0]
    half = total // 2
    wire = sbuf.dtype
    r = lax.axis_index("row")
    z = lax.axis_index("col")
    d = lax.axis_index("depth")

    def rows_of(index):
        return pl.ds(pl.multiple_of(index * block, block), block)

    def weight_copies(c):
        span = slice(None) if chunks == 1 else pl.ds(pl.multiple_of(c * width, width), width)
        return (
            pltpu.make_async_copy(gw.at[:, span], gwv.at[c], wsem.at[0, c]),
            pltpu.make_async_copy(uw.at[:, span], uwv.at[c], wsem.at[1, c]),
            pltpu.make_async_copy(dw.at[span, :], dwv.at[c], wsem.at[2, c]),
        )

    for c in range(chunks):
        for copy in weight_copies(c):
            copy.start()

    barrier = pltpu.get_barrier_semaphore()
    for k in range(1, rows):
        pl.semaphore_signal(barrier, inc=1, device_id={"row": lax.rem(r + k, rows)}, device_id_type=MESH)
    for j in range(1, depths):
        pl.semaphore_signal(barrier, inc=1, device_id={"depth": lax.rem(d + j, depths)}, device_id_type=MESH)

    @pl.when(z > 0)
    def _():
        pl.semaphore_signal(barrier, inc=1, device_id={"col": z - 1}, device_id_type=MESH)

    @pl.when(z < cols - 1)
    def _():
        pl.semaphore_signal(barrier, inc=1, device_id={"col": z + 1}, device_id_type=MESH)

    for a, (mine, everyone) in enumerate(((tok, tok_all), (cot, cot_all))):
        everyone[rows_of(r * depths + d), :] = mine[...]
    acc[...] = jnp.zeros_like(acc)

    near = (rows - 1) + (depths - 1)

    @pl.when(jnp.logical_or(z == 0, z == cols - 1))
    def _():
        pl.semaphore_wait(barrier, near + 1)

    @pl.when(jnp.logical_and(z > 0, z < cols - 1))
    def _():
        pl.semaphore_wait(barrier, near + 2)

    pairs = ((tok, tok_all), (cot, cot_all))

    def first_hop(a, k, source_row):
        mine, everyone = pairs[a]
        return pltpu.make_async_remote_copy(
            src_ref=mine,
            dst_ref=everyone.at[rows_of(source_row * depths + d), :],
            send_sem=g1_send.at[a, k - 1],
            recv_sem=g1_recv.at[a, k - 1],
            device_id={"row": lax.rem(r + k, rows)},
            device_id_type=MESH,
        )

    def second_hop(a, k, j, source_depth):
        everyone = pairs[a][1]
        where = rows_of(lax.rem(r - k + rows, rows) * depths + source_depth)
        return pltpu.make_async_remote_copy(
            src_ref=everyone.at[where, :],
            dst_ref=everyone.at[where, :],
            send_sem=g2_send.at[a, k, j - 1],
            recv_sem=g2_recv.at[a, k, j - 1],
            device_id={"depth": lax.rem(d + j, depths)},
            device_id_type=MESH,
        )

    for k in range(1, rows):
        for a in range(2):
            first_hop(a, k, r).start()
    for k in range(rows):
        for a in range(2):
            if k:
                first_hop(a, k, lax.rem(r - k + rows, rows)).wait_recv()
            for j in range(1, depths):
                second_hop(a, k, j, d).start()
    for k in range(rows):
        for a in range(2):
            for j in range(1, depths):
                second_hop(a, k, j, lax.rem(d - j + depths, depths)).wait_recv()

    def position(way):
        return z if way == 0 else cols - 1 - z

    def token_rows(way):
        return pl.ds(half, half) if way == 0 else pl.ds(0, half)

    def sum_copy(way, c):
        target = lax.rem(z + 1, cols) if way == 0 else lax.rem(z + cols - 1, cols)
        return pltpu.make_async_remote_copy(
            src_ref=sbuf.at[way, c],
            dst_ref=rbuf.at[way, c],
            send_sem=rs_send.at[way, c],
            recv_sem=rs_recv.at[way, c],
            device_id={"col": target},
            device_id_type=MESH,
        )

    def result_copy(way, c):
        target = lax.rem(z + cols - 1, cols) if way == 0 else lax.rem(z + 1, cols)
        where = res.at[c, :, token_rows(way), :]
        return pltpu.make_async_remote_copy(
            src_ref=where,
            dst_ref=where,
            send_sem=ag_send.at[way, c],
            recv_sem=ag_recv.at[way, c],
            device_id={"col": target},
            device_id_type=MESH,
        )

    def partial_sums(c):
        for copy in weight_copies(c):
            copy.wait()
        part[c, 0] = dot_nn(tok_all[...], gwv[c])
        part[c, 1] = dot_nn(tok_all[...], uwv[c])
        part[c, 2] = dot_nt(cot_all[...], dwv[c])

    def pack(value):
        return (value * jnp.abs(value)).astype(wire) if wire == BF16 else value

    def unpack(value):
        if wire != BF16:
            return value
        value = value.astype(F32)
        root = jnp.sqrt(jnp.abs(value))
        return jnp.where(value < 0, -root, root)

    def first_sum(way, c):
        sbuf[way, c] = pack(part[c, :, token_rows(way), :])
        sum_copy(way, c).start()

    def pass_sum(way, c):
        at = position(way)
        mine = token_rows(way)
        sum_copy(way, c).wait_recv()

        @pl.when(at < cols - 1)
        def _():
            sbuf[way, c] = pack(part[c, :, mine, :] + unpack(rbuf[way, c]))
            sum_copy(way, c).start()

        @pl.when(at == cols - 1)
        def _():
            gate = part[c, 0, mine, :] + unpack(rbuf[way, c, 0])
            up = part[c, 1, mine, :] + unpack(rbuf[way, c, 1])
            hidden_cot = part[c, 2, mine, :] + unpack(rbuf[way, c, 2])
            sig = jax.nn.sigmoid(gate)
            res[c, 0, mine, :] = (gate * sig * up).astype(BF16)
            res[c, 1, mine, :] = (hidden_cot * up * sig * (1.0 + gate * (1.0 - sig))).astype(BF16)
            res[c, 2, mine, :] = (hidden_cot * gate * sig).astype(BF16)
            result_copy(way, c).start()

    def pass_result(way, c):
        result_copy(way, c).wait_recv()

        @pl.when(position(way) > 0)
        def _():
            result_copy(way, c).start()

    def add_outputs(c):
        acc[0] += dot_nn(res[c, 0], dwv[c])
        acc[1] += dot_nt(res[c, 1], gwv[c]) + dot_nt(res[c, 2], uwv[c])

    last = cols - 1

    def within(c):
        return jnp.logical_and(c >= 0, c < chunks)

    def step(s, carry):
        for way in range(2):
            at = position(way)

            @pl.when(jnp.logical_and(at > 0, within(s - at)))
            def _():
                pass_sum(way, s - at)

        for way in range(2):
            at = position(way)
            c = s - last - (last - at)

            @pl.when(jnp.logical_and(at < last, within(c)))
            def _():
                pass_result(way, c)

        @pl.when(s < chunks)
        def _():
            partial_sums(s)
            for way in range(2):

                @pl.when(position(way) == 0)
                def _():
                    first_sum(way, s)

        ready = s - last - jnp.maximum(z, last - z)

        @pl.when(within(ready))
        def _():
            add_outputs(ready)

        return carry

    lax.fori_loop(0, chunks + 2 * last, step, 0)

    def depth_copy(a, row, j, target_depth):
        return pltpu.make_async_remote_copy(
            src_ref=acc.at[a, pl.ds(pl.multiple_of((row * depths + target_depth) * block, block), block), :],
            dst_ref=abuf.at[j - 1, row, a],
            send_sem=a_send.at[j - 1, row, a],
            recv_sem=a_recv.at[j - 1, row, a],
            device_id={"depth": lax.rem(d + j, depths)},
            device_id_type=MESH,
        )

    def row_copy(k):
        return pltpu.make_async_remote_copy(
            src_ref=bsend.at[k - 1],
            dst_ref=brecv.at[k - 1],
            send_sem=b_send.at[k - 1],
            recv_sem=b_recv.at[k - 1],
            device_id={"row": lax.rem(r + k, rows)},
            device_id_type=MESH,
        )

    for row in range(rows):
        for a in range(2):
            for j in range(1, depths):
                depth_copy(a, row, j, lax.rem(d + j, depths)).start()
    for row in range(rows):
        for a in range(2):
            for j in range(1, depths):
                depth_copy(a, row, j, lax.rem(d + j, depths)).wait_recv()
    for k in list(range(1, rows)) + [0]:
        row = lax.rem(r + k, rows)
        for a in range(2):
            value = acc[a, rows_of(row * depths + d), :]
            for j in range(1, depths):
                value = value + abuf[j - 1, row, a]
            if k:
                bsend[k - 1, a] = value.astype(bsend.dtype)
            else:
                own[a] = value
        if k:
            row_copy(k).start()
    for k in range(1, rows):
        row_copy(k).wait_recv()
    for a in range(2):
        value = own[a]
        for k in range(1, rows):
            value = value + brecv[k - 1, a].astype(F32)
        sums[a] = value.astype(sums.dtype)

    for k in range(1, rows):
        row_copy(k).wait_send()
        for a in range(2):
            first_hop(a, k, r).wait_send()
    for a in range(2):
        for k in range(rows):
            for j in range(1, depths):
                second_hop(a, k, j, d).wait_send()
                depth_copy(a, k, j, lax.rem(d + j, depths)).wait_send()

    def drain(c, carry):
        for way in range(2):
            at = position(way)

            @pl.when(at < cols - 1)
            def _():
                sum_copy(way, c).wait_send()

            @pl.when(at > 0)
            def _():
                result_copy(way, c).wait_send()

        return carry

    lax.fori_loop(0, chunks, drain, 0)


def grads_kernel(scale, sums, tok_all, cot_all, res, out, tgrad, gate_grad, up_grad, down_grad):
    @pl.when(pl.program_id(0) == 0)
    def _():
        out[...] = sums[0]
        tgrad[...] = sums[1]

    gate_grad[...] = (dot_tn(tok_all[...], res[0, 1]) * scale).astype(BF16)
    up_grad[...] = (dot_tn(tok_all[...], res[0, 2]) * scale).astype(BF16)
    down_grad[...] = (dot_tn(res[0, 0], cot_all[...]) * scale).astype(BF16)


def shards(rows, cols, depths, tokens, cotangent, gate_weight, up_weight, down_weight):
    block, feats = tokens.shape
    units = gate_weight.shape[1]
    total = block * rows * depths
    half = total // 2
    width = 256 if units % 256 == 0 else units
    chunks = units // width
    late = BF16 if rows <= 4 else F32
    wire = BF16 if cols <= 4 else F32
    vmem = pl.BlockSpec(memory_space=pltpu.VMEM)
    hbm = pl.BlockSpec(memory_space=pl.ANY)
    dma = pltpu.SemaphoreType.DMA
    sums, tok_all, cot_all, res = pl.pallas_call(
        functools.partial(layer_kernel, rows, cols, depths),
        out_shape=(
            jax.ShapeDtypeStruct((2, block, feats), BF16),
            jax.ShapeDtypeStruct((total, feats), BF16),
            jax.ShapeDtypeStruct((total, feats), BF16),
            jax.ShapeDtypeStruct((chunks, 3, total, width), BF16),
        ),
        in_specs=[vmem, vmem, hbm, hbm, hbm],
        out_specs=(vmem,) * 4,
        scratch_shapes=[
            pltpu.VMEM((chunks, feats, width), BF16),
            pltpu.VMEM((chunks, feats, width), BF16),
            pltpu.VMEM((chunks, width, feats), BF16),
            pltpu.VMEM((chunks, 3, total, width), F32),
            pltpu.VMEM((2, chunks, 3, half, width), wire),
            pltpu.VMEM((2, chunks, 3, half, width), wire),
            pltpu.VMEM((2, total, feats), F32),
            pltpu.VMEM((depths - 1, rows, 2, block, feats), F32),
            pltpu.VMEM((rows - 1, 2, block, feats), late),
            pltpu.VMEM((rows - 1, 2, block, feats), late),
            pltpu.VMEM((2, block, feats), F32),
            dma((3, chunks)),
            dma((2, rows - 1)),
            dma((2, rows - 1)),
            dma((2, rows, depths - 1)),
            dma((2, rows, depths - 1)),
            dma((2, chunks)),
            dma((2, chunks)),
            dma((2, chunks)),
            dma((2, chunks)),
            dma((depths - 1, rows, 2)),
            dma((depths - 1, rows, 2)),
            dma((rows - 1,)),
            dma((rows - 1,)),
        ],
        compiler_params=pltpu.CompilerParams(
            collective_id=0, has_side_effects=True, vmem_limit_bytes=VMEM_BYTES
        ),
    )(tokens, cotangent, gate_weight, up_weight, down_weight)

    whole = pl.BlockSpec((total, feats), lambda c: (0, 0))
    small = pl.BlockSpec((block, feats), lambda c: (0, 0))
    return pl.pallas_call(
        functools.partial(grads_kernel, 1.0 / math.sqrt(total)),
        out_shape=(
            jax.ShapeDtypeStruct((block, feats), BF16),
            jax.ShapeDtypeStruct((block, feats), BF16),
            jax.ShapeDtypeStruct((feats, units), BF16),
            jax.ShapeDtypeStruct((feats, units), BF16),
            jax.ShapeDtypeStruct((units, feats), BF16),
        ),
        grid=(chunks,),
        in_specs=[pl.BlockSpec((2, block, feats), lambda c: (0, 0, 0)), whole, whole, pl.BlockSpec((1, 3, total, width), lambda c: (c, 0, 0, 0))],
        out_specs=(
            small,
            small,
            pl.BlockSpec((feats, width), lambda c: (0, c)),
            pl.BlockSpec((feats, width), lambda c: (0, c)),
            pl.BlockSpec((width, feats), lambda c: (c, 0)),
        ),
        compiler_params=pltpu.CompilerParams(vmem_limit_bytes=VMEM_BYTES),
    )(sums, tok_all, cot_all, res)


def solution(mesh):
    specs = (
        P(("row", "depth"), "col"),
        P(("row", "depth"), "col"),
        P("col", ("row", "depth")),
        P("col", ("row", "depth")),
        P(("row", "depth"), "col"),
    )
    sizes = (mesh.shape["row"], mesh.shape["col"], mesh.shape["depth"])
    return jax.shard_map(
        functools.partial(shards, *sizes), mesh=mesh, in_specs=specs, out_specs=specs, check_vma=False
    )
```

```python
import functools
import math

import jax
import jax.numpy as jnp
from jax import lax
from jax.experimental import pallas as pl
from jax.experimental.pallas import tpu as pltpu
from jax.sharding import PartitionSpec as P

F32 = jnp.float32
BF16 = jnp.bfloat16
MESH = pl.DeviceIdType.MESH
VMEM_BYTES = 58 * 1024 * 1024
HOP_STEPS = 2


def dot_nn(left, right):
    return lax.dot_general(left, right, (((1,), (0,)), ((), ())), preferred_element_type=F32)


def dot_nt(left, right):
    return lax.dot_general(left, right, (((1,), (1,)), ((), ())), preferred_element_type=F32)


def dot_tn(left, right):
    return lax.dot_general(left, right, (((0,), (0,)), ((), ())), preferred_element_type=F32)


def layer_kernel(
    rows, cols, depths,
    tok, cot, gw, uw, dw,
    *refs,
):
    sums, refs = refs[:rows], refs[rows:]
    tok_all, cot_all, res, gwv, uwv, dwv, part, sbuf, rbuf, acc, abuf, *refs = refs
    wsem, g1_send, g1_recv, g2_send, g2_recv, *refs = refs
    rs_send, rs_recv, ag_send, ag_recv, a_send, a_recv = refs
    chunks, _, width = gwv.shape
    block = tok.shape[0]
    total = tok_all.shape[0]
    half = total // 2
    wire = sbuf.dtype
    r = lax.axis_index("row")
    z = lax.axis_index("col")
    d = lax.axis_index("depth")

    def rows_of(index):
        return pl.ds(pl.multiple_of(index * block, block), block)

    def weight_copies(c):
        span = slice(None) if chunks == 1 else pl.ds(pl.multiple_of(c * width, width), width)
        return (
            pltpu.make_async_copy(gw.at[:, span], gwv.at[c], wsem.at[0, c]),
            pltpu.make_async_copy(uw.at[:, span], uwv.at[c], wsem.at[1, c]),
            pltpu.make_async_copy(dw.at[span, :], dwv.at[c], wsem.at[2, c]),
        )

    for c in range(chunks):
        for copy in weight_copies(c):
            copy.start()

    barrier = pltpu.get_barrier_semaphore()
    for k in range(1, rows):
        pl.semaphore_signal(barrier, inc=1, device_id={"row": lax.rem(r + k, rows)}, device_id_type=MESH)
    for j in range(1, depths):
        pl.semaphore_signal(barrier, inc=1, device_id={"depth": lax.rem(d + j, depths)}, device_id_type=MESH)

    @pl.when(z > 0)
    def _():
        pl.semaphore_signal(barrier, inc=1, device_id={"col": z - 1}, device_id_type=MESH)

    @pl.when(z < cols - 1)
    def _():
        pl.semaphore_signal(barrier, inc=1, device_id={"col": z + 1}, device_id_type=MESH)

    for a, (mine, everyone) in enumerate(((tok, tok_all), (cot, cot_all))):
        everyone[rows_of(r * depths + d), :] = mine[...]
    acc[...] = jnp.zeros_like(acc)

    near = (rows - 1) + (depths - 1)

    @pl.when(jnp.logical_or(z == 0, z == cols - 1))
    def _():
        pl.semaphore_wait(barrier, near + 1)

    @pl.when(jnp.logical_and(z > 0, z < cols - 1))
    def _():
        pl.semaphore_wait(barrier, near + 2)

    pairs = ((tok, tok_all), (cot, cot_all))

    def first_hop(a, k, source_row):
        mine, everyone = pairs[a]
        return pltpu.make_async_remote_copy(
            src_ref=mine,
            dst_ref=everyone.at[rows_of(source_row * depths + d), :],
            send_sem=g1_send.at[a, k - 1],
            recv_sem=g1_recv.at[a, k - 1],
            device_id={"row": lax.rem(r + k, rows)},
            device_id_type=MESH,
        )

    def second_hop(a, k, j, source_depth):
        everyone = pairs[a][1]
        where = rows_of(lax.rem(r - k + rows, rows) * depths + source_depth)
        return pltpu.make_async_remote_copy(
            src_ref=everyone.at[where, :],
            dst_ref=everyone.at[where, :],
            send_sem=g2_send.at[a, k, j - 1],
            recv_sem=g2_recv.at[a, k, j - 1],
            device_id={"depth": lax.rem(d + j, depths)},
            device_id_type=MESH,
        )

    for k in range(1, rows):
        for a in range(2):
            first_hop(a, k, r).start()
    for k in range(rows):
        for a in range(2):
            if k:
                first_hop(a, k, lax.rem(r - k + rows, rows)).wait_recv()
            for j in range(1, depths):
                second_hop(a, k, j, d).start()
    for k in range(rows):
        for a in range(2):
            for j in range(1, depths):
                second_hop(a, k, j, lax.rem(d - j + depths, depths)).wait_recv()

    def position(way):
        return z if way == 0 else cols - 1 - z

    def token_rows(way):
        return pl.ds(half, half) if way == 0 else pl.ds(0, half)

    def sum_copy(way, c):
        target = lax.rem(z + 1, cols) if way == 0 else lax.rem(z + cols - 1, cols)
        return pltpu.make_async_remote_copy(
            src_ref=sbuf.at[way, c],
            dst_ref=rbuf.at[way, c],
            send_sem=rs_send.at[way, c],
            recv_sem=rs_recv.at[way, c],
            device_id={"col": target},
            device_id_type=MESH,
        )

    def result_copy(way, c):
        target = lax.rem(z + cols - 1, cols) if way == 0 else lax.rem(z + 1, cols)
        where = res.at[c, :, token_rows(way), :]
        return pltpu.make_async_remote_copy(
            src_ref=where,
            dst_ref=where,
            send_sem=ag_send.at[way, c],
            recv_sem=ag_recv.at[way, c],
            device_id={"col": target},
            device_id_type=MESH,
        )

    def partial_sums(c):
        for copy in weight_copies(c):
            copy.wait()
        part[c, 0] = dot_nn(tok_all[...], gwv[c])
        part[c, 1] = dot_nn(tok_all[...], uwv[c])
        part[c, 2] = dot_nt(cot_all[...], dwv[c])

    def pack(value):
        return (value * jnp.abs(value)).astype(wire) if wire == BF16 else value

    def unpack(value):
        if wire != BF16:
            return value
        value = value.astype(F32)
        root = jnp.sqrt(jnp.abs(value))
        return jnp.where(value < 0, -root, root)

    def first_sum(way, c):
        sbuf[way, c] = pack(part[c, :, token_rows(way), :])
        sum_copy(way, c).start()

    def pass_sum(way, c):
        at = position(way)
        mine = token_rows(way)
        sum_copy(way, c).wait_recv()

        @pl.when(at < cols - 1)
        def _():
            sbuf[way, c] = pack(part[c, :, mine, :] + unpack(rbuf[way, c]))
            sum_copy(way, c).start()

        @pl.when(at == cols - 1)
        def _():
            gate = part[c, 0, mine, :] + unpack(rbuf[way, c, 0])
            up = part[c, 1, mine, :] + unpack(rbuf[way, c, 1])
            hidden_cot = part[c, 2, mine, :] + unpack(rbuf[way, c, 2])
            sig = jax.nn.sigmoid(gate)
            res[c, 0, mine, :] = (gate * sig * up).astype(BF16)
            res[c, 1, mine, :] = (hidden_cot * up * sig * (1.0 + gate * (1.0 - sig))).astype(BF16)
            res[c, 2, mine, :] = (hidden_cot * gate * sig).astype(BF16)
            result_copy(way, c).start()

    def pass_result(way, c):
        result_copy(way, c).wait_recv()

        @pl.when(position(way) > 0)
        def _():
            result_copy(way, c).start()

    def add_outputs(c):
        acc[0] += dot_nn(res[c, 0], dwv[c])
        acc[1] += dot_nt(res[c, 1], gwv[c]) + dot_nt(res[c, 2], uwv[c])

    last = cols - 1

    def within(c):
        return jnp.logical_and(c >= 0, c < chunks)

    def step(s, carry):
        for way in range(2):
            at = position(way)

            @pl.when(jnp.logical_and(at > 0, within(s - HOP_STEPS * at)))
            def _():
                pass_sum(way, s - HOP_STEPS * at)

        for way in range(2):
            at = position(way)
            c = s - HOP_STEPS * (last + last - at)

            @pl.when(jnp.logical_and(at < last, within(c)))
            def _():
                pass_result(way, c)

        @pl.when(s < chunks)
        def _():
            partial_sums(s)
            for way in range(2):

                @pl.when(position(way) == 0)
                def _():
                    first_sum(way, s)

        ready = s - HOP_STEPS * (last + jnp.maximum(z, last - z))

        @pl.when(within(ready))
        def _():
            add_outputs(ready)

        return carry

    lax.fori_loop(0, chunks + HOP_STEPS * 2 * last, step, 0)

    def depth_copy(a, row, j, target_depth):
        return pltpu.make_async_remote_copy(
            src_ref=acc.at[a, pl.ds(pl.multiple_of((row * depths + target_depth) * block, block), block), :],
            dst_ref=abuf.at[j - 1, row, a],
            send_sem=a_send.at[j - 1, row, a],
            recv_sem=a_recv.at[j - 1, row, a],
            device_id={"depth": lax.rem(d + j, depths)},
            device_id_type=MESH,
        )

    for row in range(rows):
        for a in range(2):
            for j in range(1, depths):
                depth_copy(a, row, j, lax.rem(d + j, depths)).start()
    for row in range(rows):
        for a in range(2):
            for j in range(1, depths):
                depth_copy(a, row, j, lax.rem(d + j, depths)).wait_recv()
    for k in range(rows):
        row = lax.rem(r + k, rows)
        for a in range(2):
            value = acc[a, rows_of(row * depths + d), :]
            for j in range(1, depths):
                value = value + abuf[j - 1, row, a]
            sums[k][a] = value.astype(sums[k].dtype)

    for k in range(1, rows):
        for a in range(2):
            first_hop(a, k, r).wait_send()
    for a in range(2):
        for k in range(rows):
            for j in range(1, depths):
                second_hop(a, k, j, d).wait_send()
                depth_copy(a, k, j, lax.rem(d + j, depths)).wait_send()

    def drain(c, carry):
        for way in range(2):
            at = position(way)

            @pl.when(at < cols - 1)
            def _():
                sum_copy(way, c).wait_send()

            @pl.when(at > 0)
            def _():
                result_copy(way, c).wait_send()

        return carry

    lax.fori_loop(0, chunks, drain, 0)


def grads_kernel(scale, tok_all, cot_all, res, gate_grad, up_grad, down_grad, tok_t):
    @pl.when(pl.program_id(0) == 0)
    def _():
        tok_t[...] = tok_all[...].T

    gate_grad[...] = (dot_nn(tok_t[...], res[0, 1]) * scale).astype(BF16)
    up_grad[...] = (dot_nn(tok_t[...], res[0, 2]) * scale).astype(BF16)
    down_grad[...] = (dot_tn(res[0, 0], cot_all[...]) * scale).astype(BF16)


def shards(rows, cols, depths, tokens, cotangent, gate_weight, up_weight, down_weight):
    block, feats = tokens.shape
    units = gate_weight.shape[1]
    total = block * rows * depths
    half = total // 2
    width = 256 if units % 256 == 0 else units
    chunks = units // width
    late = BF16 if rows <= 4 else F32
    wire = BF16 if cols <= 4 else F32
    vmem = pl.BlockSpec(memory_space=pltpu.VMEM)
    hbm = pl.BlockSpec(memory_space=pl.ANY)
    dma = pltpu.SemaphoreType.DMA
    *sums, tok_all, cot_all, res = pl.pallas_call(
        functools.partial(layer_kernel, rows, cols, depths),
        out_shape=(
            jax.ShapeDtypeStruct((2, block, feats), F32),
            *[jax.ShapeDtypeStruct((2, block, feats), late)] * (rows - 1),
            jax.ShapeDtypeStruct((total, feats), BF16),
            jax.ShapeDtypeStruct((total, feats), BF16),
            jax.ShapeDtypeStruct((chunks, 3, total, width), BF16),
        ),
        in_specs=[vmem, vmem, hbm, hbm, hbm],
        out_specs=(vmem,) * (rows + 3),
        scratch_shapes=[
            pltpu.VMEM((chunks, feats, width), BF16),
            pltpu.VMEM((chunks, feats, width), BF16),
            pltpu.VMEM((chunks, width, feats), BF16),
            pltpu.VMEM((chunks, 3, total, width), F32),
            pltpu.VMEM((2, chunks, 3, half, width), wire),
            pltpu.VMEM((2, chunks, 3, half, width), wire),
            pltpu.VMEM((2, total, feats), F32),
            pltpu.VMEM((depths - 1, rows, 2, block, feats), F32),
            dma((3, chunks)),
            dma((2, rows - 1)),
            dma((2, rows - 1)),
            dma((2, rows, depths - 1)),
            dma((2, rows, depths - 1)),
            dma((2, chunks)),
            dma((2, chunks)),
            dma((2, chunks)),
            dma((2, chunks)),
            dma((depths - 1, rows, 2)),
            dma((depths - 1, rows, 2)),
        ],
        compiler_params=pltpu.CompilerParams(
            collective_id=0, has_side_effects=True, vmem_limit_bytes=VMEM_BYTES
        ),
    )(tokens, cotangent, gate_weight, up_weight, down_weight)

    arrived = []
    for k in range(1, rows):
        ring = [(i, (i + k) % rows) for i in range(rows)]
        arrived.append(lax.ppermute(sums[k], "row", ring))
    out, tgrad = (
        sum((part[a].astype(F32) for part in arrived), sums[0][a]).astype(BF16) for a in range(2)
    )

    whole = pl.BlockSpec((total, feats), lambda c: (0, 0))
    gate_grad, up_grad, down_grad = pl.pallas_call(
        functools.partial(grads_kernel, 1.0 / math.sqrt(total)),
        out_shape=(
            jax.ShapeDtypeStruct((feats, units), BF16),
            jax.ShapeDtypeStruct((feats, units), BF16),
            jax.ShapeDtypeStruct((units, feats), BF16),
        ),
        grid=(chunks,),
        in_specs=[whole, whole, pl.BlockSpec((1, 3, total, width), lambda c: (c, 0, 0, 0))],
        out_specs=(
            pl.BlockSpec((feats, width), lambda c: (0, c)),
            pl.BlockSpec((feats, width), lambda c: (0, c)),
            pl.BlockSpec((width, feats), lambda c: (c, 0)),
        ),
        scratch_shapes=[pltpu.VMEM((feats, total), BF16)],
        cost_estimate=pl.CostEstimate(
            flops=6 * total * feats * units, bytes_accessed=6 * feats * units, transcendentals=0
        ),
        compiler_params=pltpu.CompilerParams(vmem_limit_bytes=VMEM_BYTES),
    )(tok_all, cot_all, res)
    return (out, tgrad, gate_grad, up_grad, down_grad)


def solution(mesh):
    specs = (
        P(("row", "depth"), "col"),
        P(("row", "depth"), "col"),
        P("col", ("row", "depth")),
        P("col", ("row", "depth")),
        P(("row", "depth"), "col"),
    )
    sizes = (mesh.shape["row"], mesh.shape["col"], mesh.shape["depth"])
    return jax.shard_map(
        functools.partial(shards, *sizes), mesh=mesh, in_specs=specs, out_specs=specs, check_vma=False
    )
```

```python
import functools
import math

import jax
import jax.numpy as jnp
from jax import lax
from jax.experimental import pallas as pl
from jax.experimental.pallas import tpu as pltpu
from jax.sharding import PartitionSpec as P

F32 = jnp.float32
BF16 = jnp.bfloat16
MESH = pl.DeviceIdType.MESH
VMEM_BYTES = 58 * 1024 * 1024
HOP_STEPS = 3
PIECES = 2


def dot_nn(left, right):
    return lax.dot_general(left, right, (((1,), (0,)), ((), ())), preferred_element_type=F32)


def dot_nt(left, right):
    return lax.dot_general(left, right, (((1,), (1,)), ((), ())), preferred_element_type=F32)


def dot_tn(left, right):
    return lax.dot_general(left, right, (((0,), (0,)), ((), ())), preferred_element_type=F32)


def layer_kernel(
    rows, cols, depths,
    tok, cot, gw, uw, dw,
    *refs,
):
    sums, refs = refs[:rows], refs[rows:]
    tok_all, cot_all, res, gwv, uwv, dwv, part, sbuf, rbuf, acc, abuf, *refs = refs
    wsem, g1_send, g1_recv, g2_send, g2_recv, *refs = refs
    rs_send, rs_recv, ag_send, ag_recv, a_send, a_recv = refs
    chunks, _, width = gwv.shape
    block = tok.shape[0]
    total = tok_all.shape[0]
    half = total // 2
    piece = half // PIECES
    count = chunks * PIECES
    wire = sbuf.dtype
    r = lax.axis_index("row")
    z = lax.axis_index("col")
    d = lax.axis_index("depth")

    def rows_of(index):
        return pl.ds(pl.multiple_of(index * block, block), block)

    def weight_copies(c):
        span = slice(None) if chunks == 1 else pl.ds(pl.multiple_of(c * width, width), width)
        return (
            pltpu.make_async_copy(gw.at[:, span], gwv.at[c], wsem.at[0, c]),
            pltpu.make_async_copy(uw.at[:, span], uwv.at[c], wsem.at[1, c]),
            pltpu.make_async_copy(dw.at[span, :], dwv.at[c], wsem.at[2, c]),
        )

    for c in range(chunks):
        for copy in weight_copies(c):
            copy.start()

    barrier = pltpu.get_barrier_semaphore()
    for k in range(1, rows):
        pl.semaphore_signal(barrier, inc=1, device_id={"row": lax.rem(r + k, rows)}, device_id_type=MESH)
    for j in range(1, depths):
        pl.semaphore_signal(barrier, inc=1, device_id={"depth": lax.rem(d + j, depths)}, device_id_type=MESH)

    @pl.when(z > 0)
    def _():
        pl.semaphore_signal(barrier, inc=1, device_id={"col": z - 1}, device_id_type=MESH)

    @pl.when(z < cols - 1)
    def _():
        pl.semaphore_signal(barrier, inc=1, device_id={"col": z + 1}, device_id_type=MESH)

    for a, (mine, everyone) in enumerate(((tok, tok_all), (cot, cot_all))):
        everyone[rows_of(r * depths + d), :] = mine[...]
    acc[...] = jnp.zeros_like(acc)

    near = (rows - 1) + (depths - 1)

    @pl.when(jnp.logical_or(z == 0, z == cols - 1))
    def _():
        pl.semaphore_wait(barrier, near + 1)

    @pl.when(jnp.logical_and(z > 0, z < cols - 1))
    def _():
        pl.semaphore_wait(barrier, near + 2)

    pairs = ((tok, tok_all), (cot, cot_all))

    def first_hop(a, k, source_row):
        mine, everyone = pairs[a]
        return pltpu.make_async_remote_copy(
            src_ref=mine,
            dst_ref=everyone.at[rows_of(source_row * depths + d), :],
            send_sem=g1_send.at[a, k - 1],
            recv_sem=g1_recv.at[a, k - 1],
            device_id={"row": lax.rem(r + k, rows)},
            device_id_type=MESH,
        )

    def second_hop(a, k, j, source_depth):
        everyone = pairs[a][1]
        where = rows_of(lax.rem(r - k + rows, rows) * depths + source_depth)
        return pltpu.make_async_remote_copy(
            src_ref=everyone.at[where, :],
            dst_ref=everyone.at[where, :],
            send_sem=g2_send.at[a, k, j - 1],
            recv_sem=g2_recv.at[a, k, j - 1],
            device_id={"depth": lax.rem(d + j, depths)},
            device_id_type=MESH,
        )

    for k in range(1, rows):
        for a in range(2):
            first_hop(a, k, r).start()
    for k in range(rows):
        for a in range(2):
            if k:
                first_hop(a, k, lax.rem(r - k + rows, rows)).wait_recv()
            for j in range(1, depths):
                second_hop(a, k, j, d).start()
    for k in range(rows):
        for a in range(2):
            for j in range(1, depths):
                second_hop(a, k, j, lax.rem(d - j + depths, depths)).wait_recv()

    def position(way):
        return z if way == 0 else cols - 1 - z

    def place(way, u):
        base = half if way == 0 else 0
        rows_at = pl.multiple_of(base + lax.rem(u, PIECES) * piece, piece)
        return lax.div(u, PIECES), pl.ds(rows_at, piece)

    def sum_copy(way, u):
        target = lax.rem(z + 1, cols) if way == 0 else lax.rem(z + cols - 1, cols)
        return pltpu.make_async_remote_copy(
            src_ref=sbuf.at[way, u],
            dst_ref=rbuf.at[way, u],
            send_sem=rs_send.at[way, u],
            recv_sem=rs_recv.at[way, u],
            device_id={"col": target},
            device_id_type=MESH,
        )

    def result_copy(way, u):
        target = lax.rem(z + cols - 1, cols) if way == 0 else lax.rem(z + 1, cols)
        c, mine = place(way, u)
        where = res.at[c, :, mine, :]
        return pltpu.make_async_remote_copy(
            src_ref=where,
            dst_ref=where,
            send_sem=ag_send.at[way, u],
            recv_sem=ag_recv.at[way, u],
            device_id={"col": target},
            device_id_type=MESH,
        )

    def partial_sums(c):
        for copy in weight_copies(c):
            copy.wait()
        part[c, 0] = dot_nn(tok_all[...], gwv[c])
        part[c, 1] = dot_nn(tok_all[...], uwv[c])
        part[c, 2] = dot_nt(cot_all[...], dwv[c])

    def pack(value):
        return (value * jnp.abs(value)).astype(wire) if wire == BF16 else value

    def unpack(value):
        if wire != BF16:
            return value
        value = value.astype(F32)
        root = jnp.sqrt(jnp.abs(value))
        return jnp.where(value < 0, -root, root)

    def first_sum(way, u):
        c, mine = place(way, u)
        sbuf[way, u] = pack(part[c, :, mine, :])
        sum_copy(way, u).start()

    def pass_sum(way, u):
        at = position(way)
        c, mine = place(way, u)
        sum_copy(way, u).wait_recv()

        @pl.when(at < cols - 1)
        def _():
            sbuf[way, u] = pack(part[c, :, mine, :] + unpack(rbuf[way, u]))
            sum_copy(way, u).start()

        @pl.when(at == cols - 1)
        def _():
            gate = part[c, 0, mine, :] + unpack(rbuf[way, u, 0])
            up = part[c, 1, mine, :] + unpack(rbuf[way, u, 1])
            hidden_cot = part[c, 2, mine, :] + unpack(rbuf[way, u, 2])
            sig = jax.nn.sigmoid(gate)
            res[c, 0, mine, :] = (gate * sig * up).astype(BF16)
            res[c, 1, mine, :] = (hidden_cot * up * sig * (1.0 + gate * (1.0 - sig))).astype(BF16)
            res[c, 2, mine, :] = (hidden_cot * gate * sig).astype(BF16)
            result_copy(way, u).start()

    def pass_result(way, u):
        result_copy(way, u).wait_recv()

        @pl.when(position(way) > 0)
        def _():
            result_copy(way, u).start()

    def add_outputs(c):
        acc[0] += dot_nn(res[c, 0], dwv[c])
        acc[1] += dot_nt(res[c, 1], gwv[c]) + dot_nt(res[c, 2], uwv[c])

    last = cols - 1

    def within(u):
        return jnp.logical_and(u >= 0, u < count)

    def step(s, carry):
        for way in range(2):
            at = position(way)
            u = s - HOP_STEPS * at

            @pl.when(jnp.logical_and(at > 0, within(u)))
            def _():
                pass_sum(way, u)

        for way in range(2):
            at = position(way)
            u = s - HOP_STEPS * (last + last - at)

            @pl.when(jnp.logical_and(at < last, within(u)))
            def _():
                pass_result(way, u)

        @pl.when(jnp.logical_and(s < count, lax.rem(s, PIECES) == 0))
        def _():
            partial_sums(lax.div(s, PIECES))
            for way in range(2):

                @pl.when(position(way) == 0)
                def _():
                    for h in range(PIECES):
                        first_sum(way, s + h)

        ready = s - HOP_STEPS * (last + jnp.maximum(z, last - z))

        @pl.when(jnp.logical_and(within(ready), lax.rem(ready + PIECES, PIECES) == PIECES - 1))
        def _():
            add_outputs(lax.div(ready, PIECES))

        return carry

    lax.fori_loop(0, count + HOP_STEPS * 2 * last, step, 0)

    def depth_copy(a, row, j, target_depth):
        return pltpu.make_async_remote_copy(
            src_ref=acc.at[a, pl.ds(pl.multiple_of((row * depths + target_depth) * block, block), block), :],
            dst_ref=abuf.at[j - 1, row, a],
            send_sem=a_send.at[j - 1, row, a],
            recv_sem=a_recv.at[j - 1, row, a],
            device_id={"depth": lax.rem(d + j, depths)},
            device_id_type=MESH,
        )

    for row in range(rows):
        for a in range(2):
            for j in range(1, depths):
                depth_copy(a, row, j, lax.rem(d + j, depths)).start()
    for row in range(rows):
        for a in range(2):
            for j in range(1, depths):
                depth_copy(a, row, j, lax.rem(d + j, depths)).wait_recv()
    for k in range(rows):
        row = lax.rem(r + k, rows)
        for a in range(2):
            value = acc[a, rows_of(row * depths + d), :]
            for j in range(1, depths):
                value = value + abuf[j - 1, row, a]
            sums[k][a] = value.astype(sums[k].dtype)

    for k in range(1, rows):
        for a in range(2):
            first_hop(a, k, r).wait_send()
    for a in range(2):
        for k in range(rows):
            for j in range(1, depths):
                second_hop(a, k, j, d).wait_send()
                depth_copy(a, k, j, lax.rem(d + j, depths)).wait_send()

    def drain(u, carry):
        for way in range(2):
            at = position(way)

            @pl.when(at < cols - 1)
            def _():
                sum_copy(way, u).wait_send()

            @pl.when(at > 0)
            def _():
                result_copy(way, u).wait_send()

        return carry

    lax.fori_loop(0, count, drain, 0)


def grads_kernel(scale, tok, cot_all, res, gate_grad, up_grad, down_grad, hidden_t):
    chunks, _, _, width = res.shape
    i = pl.program_id(0)

    @pl.when(i == 0)
    def _():
        for c in range(chunks):
            hidden_t[pl.ds(c * width, width), :] = res[c, 0].T

    tok_t = tok[...].T
    for c in range(chunks):
        span = pl.ds(c * width, width)
        gate_grad[:, span] = (dot_nn(tok_t, res[c, 1]) * scale).astype(BF16)
        up_grad[:, span] = (dot_nn(tok_t, res[c, 2]) * scale).astype(BF16)
    size = down_grad.shape[0]
    mine = hidden_t[pl.ds(pl.multiple_of(i * size, size), size), :]
    down_grad[...] = (dot_nn(mine, cot_all[...]) * scale).astype(BF16)


def shards(rows, cols, depths, tokens, cotangent, gate_weight, up_weight, down_weight):
    block, feats = tokens.shape
    units = gate_weight.shape[1]
    total = block * rows * depths
    half = total // 2
    width = 256 if units % 256 == 0 else units
    chunks = units // width
    count = chunks * PIECES
    late = BF16 if rows <= 4 else F32
    wire = BF16 if cols <= 4 else F32
    vmem = pl.BlockSpec(memory_space=pltpu.VMEM)
    hbm = pl.BlockSpec(memory_space=pl.ANY)
    dma = pltpu.SemaphoreType.DMA
    *sums, tok_all, cot_all, res = pl.pallas_call(
        functools.partial(layer_kernel, rows, cols, depths),
        out_shape=(
            jax.ShapeDtypeStruct((2, block, feats), F32),
            *[jax.ShapeDtypeStruct((2, block, feats), late)] * (rows - 1),
            jax.ShapeDtypeStruct((total, feats), BF16),
            jax.ShapeDtypeStruct((total, feats), BF16),
            jax.ShapeDtypeStruct((chunks, 3, total, width), BF16),
        ),
        in_specs=[vmem, vmem, hbm, hbm, hbm],
        out_specs=(vmem,) * (rows + 3),
        scratch_shapes=[
            pltpu.VMEM((chunks, feats, width), BF16),
            pltpu.VMEM((chunks, feats, width), BF16),
            pltpu.VMEM((chunks, width, feats), BF16),
            pltpu.VMEM((chunks, 3, total, width), F32),
            pltpu.VMEM((2, count, 3, half // PIECES, width), wire),
            pltpu.VMEM((2, count, 3, half // PIECES, width), wire),
            pltpu.VMEM((2, total, feats), F32),
            pltpu.VMEM((depths - 1, rows, 2, block, feats), F32),
            dma((3, chunks)),
            dma((2, rows - 1)),
            dma((2, rows - 1)),
            dma((2, rows, depths - 1)),
            dma((2, rows, depths - 1)),
            dma((2, count)),
            dma((2, count)),
            dma((2, count)),
            dma((2, count)),
            dma((depths - 1, rows, 2)),
            dma((depths - 1, rows, 2)),
        ],
        compiler_params=pltpu.CompilerParams(
            collective_id=0, has_side_effects=True, vmem_limit_bytes=VMEM_BYTES
        ),
    )(tokens, cotangent, gate_weight, up_weight, down_weight)

    arrived = []
    for k in range(1, rows):
        ring = [(i, (i + k) % rows) for i in range(rows)]
        arrived.append(lax.ppermute(sums[k], "row", ring))
    out, tgrad = (
        sum((part[a].astype(F32) for part in arrived), sums[0][a]).astype(BF16) for a in range(2)
    )

    steps = max(n for n in (8, 4, 2, 1) if feats % (128 * n) == 0 and units % (16 * n) == 0)
    gate_grad, up_grad, down_grad = pl.pallas_call(
        functools.partial(grads_kernel, 1.0 / math.sqrt(total)),
        out_shape=(
            jax.ShapeDtypeStruct((feats, units), BF16),
            jax.ShapeDtypeStruct((feats, units), BF16),
            jax.ShapeDtypeStruct((units, feats), BF16),
        ),
        grid=(steps,),
        in_specs=[
            pl.BlockSpec((total, feats // steps), lambda i: (0, i)),
            pl.BlockSpec((total, feats), lambda i: (0, 0)),
            pl.BlockSpec((chunks, 3, total, width), lambda i: (0, 0, 0, 0)),
        ],
        out_specs=(
            pl.BlockSpec((feats // steps, units), lambda i: (i, 0)),
            pl.BlockSpec((feats // steps, units), lambda i: (i, 0)),
            pl.BlockSpec((units // steps, feats), lambda i: (i, 0)),
        ),
        scratch_shapes=[pltpu.VMEM((units, total), BF16)],
        cost_estimate=pl.CostEstimate(
            flops=6 * total * feats * units, bytes_accessed=6 * feats * units, transcendentals=0
        ),
        compiler_params=pltpu.CompilerParams(vmem_limit_bytes=VMEM_BYTES),
    )(tok_all, cot_all, res)
    return (out, tgrad, gate_grad, up_grad, down_grad)


def solution(mesh):
    specs = (
        P(("row", "depth"), "col"),
        P(("row", "depth"), "col"),
        P("col", ("row", "depth")),
        P("col", ("row", "depth")),
        P(("row", "depth"), "col"),
    )
    sizes = (mesh.shape["row"], mesh.shape["col"], mesh.shape["depth"])
    return jax.shard_map(
        functools.partial(shards, *sizes), mesh=mesh, in_specs=specs, out_specs=specs, check_vma=False
    )
```

```python
import functools
import math

import jax
import jax.numpy as jnp
from jax import lax
from jax.experimental import pallas as pl
from jax.experimental.pallas import tpu as pltpu
from jax.sharding import PartitionSpec as P

F32 = jnp.float32
BF16 = jnp.bfloat16
MESH = pl.DeviceIdType.MESH
VMEM_BYTES = 42 * 1024 * 1024
GRADS_VMEM_BYTES = 18 * 1024 * 1024
EARLY = 3
HOP_STEPS = 3
PIECES = 2


def dot_nn(left, right):
    return lax.dot_general(left, right, (((1,), (0,)), ((), ())), preferred_element_type=F32)


def dot_nt(left, right):
    return lax.dot_general(left, right, (((1,), (1,)), ((), ())), preferred_element_type=F32)


def dot_tn(left, right):
    return lax.dot_general(left, right, (((0,), (0,)), ((), ())), preferred_element_type=F32)


def layer_kernel(
    rows, cols, depths,
    tok, cot, gw, uw, dw,
    *refs,
):
    sums, refs = refs[:rows], refs[rows:]
    tok_all, cot_all, res, gwv, uwv, dwv, part, sbuf, rbuf, acc, abuf, *refs = refs
    wsem, g1_send, g1_recv, g2_send, g2_recv, *refs = refs
    rs_send, rs_recv, ag_send, ag_recv, a_send, a_recv = refs
    chunks, _, width = gwv.shape
    block = tok.shape[0]
    total = tok_all.shape[0]
    half = total // 2
    piece = half // PIECES
    count = chunks * PIECES
    wire = sbuf.dtype
    r = lax.axis_index("row")
    z = lax.axis_index("col")
    d = lax.axis_index("depth")

    def rows_of(index):
        return pl.ds(pl.multiple_of(index * block, block), block)

    def weight_copies(c):
        span = slice(None) if chunks == 1 else pl.ds(pl.multiple_of(c * width, width), width)
        return (
            pltpu.make_async_copy(gw.at[:, span], gwv.at[c], wsem.at[0, c]),
            pltpu.make_async_copy(uw.at[:, span], uwv.at[c], wsem.at[1, c]),
            pltpu.make_async_copy(dw.at[span, :], dwv.at[c], wsem.at[2, c]),
        )

    for c in range(chunks):
        for copy in weight_copies(c):
            copy.start()

    barrier = pltpu.get_barrier_semaphore()
    for k in range(1, rows):
        pl.semaphore_signal(barrier, inc=1, device_id={"row": lax.rem(r + k, rows)}, device_id_type=MESH)
    for j in range(1, depths):
        pl.semaphore_signal(barrier, inc=1, device_id={"depth": lax.rem(d + j, depths)}, device_id_type=MESH)

    @pl.when(z > 0)
    def _():
        pl.semaphore_signal(barrier, inc=1, device_id={"col": z - 1}, device_id_type=MESH)

    @pl.when(z < cols - 1)
    def _():
        pl.semaphore_signal(barrier, inc=1, device_id={"col": z + 1}, device_id_type=MESH)

    for a, (mine, everyone) in enumerate(((tok, tok_all), (cot, cot_all))):
        everyone[rows_of(r * depths + d), :] = mine[...]
    acc[...] = jnp.zeros_like(acc)

    near = (rows - 1) + (depths - 1)

    @pl.when(jnp.logical_or(z == 0, z == cols - 1))
    def _():
        pl.semaphore_wait(barrier, near + 1)

    @pl.when(jnp.logical_and(z > 0, z < cols - 1))
    def _():
        pl.semaphore_wait(barrier, near + 2)

    pairs = ((tok, tok_all), (cot, cot_all))

    def first_hop(a, k, source_row):
        mine, everyone = pairs[a]
        return pltpu.make_async_remote_copy(
            src_ref=mine,
            dst_ref=everyone.at[rows_of(source_row * depths + d), :],
            send_sem=g1_send.at[a, k - 1],
            recv_sem=g1_recv.at[a, k - 1],
            device_id={"row": lax.rem(r + k, rows)},
            device_id_type=MESH,
        )

    def second_hop(a, k, j, source_depth):
        everyone = pairs[a][1]
        where = rows_of(lax.rem(r - k + rows, rows) * depths + source_depth)
        return pltpu.make_async_remote_copy(
            src_ref=everyone.at[where, :],
            dst_ref=everyone.at[where, :],
            send_sem=g2_send.at[a, k, j - 1],
            recv_sem=g2_recv.at[a, k, j - 1],
            device_id={"depth": lax.rem(d + j, depths)},
            device_id_type=MESH,
        )

    def gather(a):
        for k in range(rows):
            if k:
                first_hop(a, k, lax.rem(r - k + rows, rows)).wait_recv()
            for j in range(1, depths):
                second_hop(a, k, j, d).start()
        for k in range(rows):
            for j in range(1, depths):
                second_hop(a, k, j, lax.rem(d - j + depths, depths)).wait_recv()

    for a in range(2):
        for k in range(1, rows):
            first_hop(a, k, r).start()
    gather(0)

    def position(way):
        return z if way == 0 else cols - 1 - z

    def place(way, u):
        base = half if way == 0 else 0
        rows_at = pl.multiple_of(base + lax.rem(u, PIECES) * piece, piece)
        return lax.div(u, PIECES), pl.ds(rows_at, piece)

    spans = (pl.ds(0, 2), pl.ds(2, 1))

    def sum_copy(way, u, g):
        target = lax.rem(z + 1, cols) if way == 0 else lax.rem(z + cols - 1, cols)
        return pltpu.make_async_remote_copy(
            src_ref=sbuf.at[way, u, spans[g]],
            dst_ref=rbuf.at[way, u, spans[g]],
            send_sem=rs_send.at[way, u, g],
            recv_sem=rs_recv.at[way, u, g],
            device_id={"col": target},
            device_id_type=MESH,
        )

    def result_copy(way, u):
        target = lax.rem(z + cols - 1, cols) if way == 0 else lax.rem(z + 1, cols)
        c, mine = place(way, u)
        where = res.at[c, :, mine, :]
        return pltpu.make_async_remote_copy(
            src_ref=where,
            dst_ref=where,
            send_sem=ag_send.at[way, u],
            recv_sem=ag_recv.at[way, u],
            device_id={"col": target},
            device_id_type=MESH,
        )

    def gate_up_sums(c):
        for copy in weight_copies(c)[:2]:
            copy.wait()
        part[c, 0] = dot_nn(tok_all[...], gwv[c])
        part[c, 1] = dot_nn(tok_all[...], uwv[c])

    def cot_sums(c):
        weight_copies(c)[2].wait()
        part[c, 2] = dot_nt(cot_all[...], dwv[c])

    def pack(value):
        return (value * jnp.abs(value)).astype(wire) if wire == BF16 else value

    def unpack(value):
        if wire != BF16:
            return value
        value = value.astype(F32)
        root = jnp.sqrt(jnp.abs(value))
        return jnp.where(value < 0, -root, root)

    def first_sums(c, g):
        for way in range(2):

            @pl.when(position(way) == 0)
            def _():
                for h in range(PIECES):
                    u = c * PIECES + h
                    mine = place(way, u)[1]
                    sbuf[way, u, spans[g]] = pack(part[c, spans[g], mine, :])
                    sum_copy(way, u, g).start()

    def pass_sum(way, u):
        at = position(way)
        c, mine = place(way, u)
        for g in range(2):
            sum_copy(way, u, g).wait_recv()

        @pl.when(at < cols - 1)
        def _():
            sbuf[way, u] = pack(part[c, :, mine, :] + unpack(rbuf[way, u]))
            for g in range(2):
                sum_copy(way, u, g).start()

        @pl.when(at == cols - 1)
        def _():
            gate = part[c, 0, mine, :] + unpack(rbuf[way, u, 0])
            up = part[c, 1, mine, :] + unpack(rbuf[way, u, 1])
            hidden_cot = part[c, 2, mine, :] + unpack(rbuf[way, u, 2])
            sig = jax.nn.sigmoid(gate)
            res[c, 0, mine, :] = (gate * sig * up).astype(BF16)
            res[c, 1, mine, :] = (hidden_cot * up * sig * (1.0 + gate * (1.0 - sig))).astype(BF16)
            res[c, 2, mine, :] = (hidden_cot * gate * sig).astype(BF16)
            result_copy(way, u).start()

    def pass_result(way, u):
        result_copy(way, u).wait_recv()

        @pl.when(position(way) > 0)
        def _():
            result_copy(way, u).start()

    def depth_copy(a, row, j, target_depth):
        return pltpu.make_async_remote_copy(
            src_ref=acc.at[a, pl.ds(pl.multiple_of((row * depths + target_depth) * block, block), block), :],
            dst_ref=abuf.at[j - 1, row, a],
            send_sem=a_send.at[j - 1, row, a],
            recv_sem=a_recv.at[j - 1, row, a],
            device_id={"depth": lax.rem(d + j, depths)},
            device_id_type=MESH,
        )

    def send_output(a):
        for row in range(rows):
            for j in range(1, depths):
                depth_copy(a, row, j, lax.rem(d + j, depths)).start()

    def add_outputs(c):
        acc[0] += dot_nn(res[c, 0], dwv[c])

        @pl.when(c == chunks - 1)
        def _():
            send_output(0)

        acc[1] += dot_nt(res[c, 1], gwv[c]) + dot_nt(res[c, 2], uwv[c])

    last = cols - 1

    def within(u):
        return jnp.logical_and(u >= 0, u < count)

    def step(s, carry):
        for way in range(2):
            at = position(way)
            u = s - HOP_STEPS * at

            @pl.when(jnp.logical_and(at > 0, within(u)))
            def _():
                pass_sum(way, u)

        for way in range(2):
            at = position(way)
            u = s - HOP_STEPS * (last + last - at)

            @pl.when(jnp.logical_and(at < last, within(u)))
            def _():
                pass_result(way, u)

        @pl.when(jnp.logical_and(s < count, lax.rem(s, PIECES) == 0))
        def _():
            c = lax.div(s, PIECES)

            @pl.when(c >= early)
            def _():
                gate_up_sums(c)
                first_sums(c, 0)

            cot_sums(c)
            first_sums(c, 1)

        ready = s - HOP_STEPS * (last + jnp.maximum(z, last - z))

        @pl.when(jnp.logical_and(within(ready), lax.rem(ready + PIECES, PIECES) == PIECES - 1))
        def _():
            add_outputs(lax.div(ready, PIECES))

        return carry

    early = min(EARLY, chunks)

    def head(c, carry):
        gate_up_sums(c)
        first_sums(c, 0)
        return carry

    lax.fori_loop(0, early, head, 0)
    gather(1)
    lax.fori_loop(0, count + HOP_STEPS * 2 * last, step, 0)

    send_output(1)
    for row in range(rows):
        for a in range(2):
            for j in range(1, depths):
                depth_copy(a, row, j, lax.rem(d + j, depths)).wait_recv()
    for k in range(rows):
        row = lax.rem(r + k, rows)
        for a in range(2):
            value = acc[a, rows_of(row * depths + d), :]
            for j in range(1, depths):
                value = value + abuf[j - 1, row, a]
            sums[k][a] = value.astype(sums[k].dtype)

    for k in range(1, rows):
        for a in range(2):
            first_hop(a, k, r).wait_send()
    for a in range(2):
        for k in range(rows):
            for j in range(1, depths):
                second_hop(a, k, j, d).wait_send()
                depth_copy(a, k, j, lax.rem(d + j, depths)).wait_send()

    def drain(u, carry):
        for way in range(2):
            at = position(way)

            @pl.when(at < cols - 1)
            def _():
                for g in range(2):
                    sum_copy(way, u, g).wait_send()

            @pl.when(at > 0)
            def _():
                result_copy(way, u).wait_send()

        return carry

    lax.fori_loop(0, count, drain, 0)


def grads_kernel(scale, tok, cot_all, res, gate_grad, up_grad, down_grad, hidden_t):
    chunks, _, _, width = res.shape
    i = pl.program_id(0)

    @pl.when(i == 0)
    def _():
        for c in range(chunks):
            hidden_t[pl.ds(c * width, width), :] = res[c, 0].T

    tok_t = tok[...].T
    for c in range(chunks):
        span = pl.ds(c * width, width)
        gate_grad[:, span] = (dot_nn(tok_t, res[c, 1]) * scale).astype(BF16)
        up_grad[:, span] = (dot_nn(tok_t, res[c, 2]) * scale).astype(BF16)
    size = down_grad.shape[0]
    mine = hidden_t[pl.ds(pl.multiple_of(i * size, size), size), :]
    down_grad[...] = (dot_nn(mine, cot_all[...]) * scale).astype(BF16)


def shards(rows, cols, depths, tokens, cotangent, gate_weight, up_weight, down_weight):
    block, feats = tokens.shape
    units = gate_weight.shape[1]
    total = block * rows * depths
    half = total // 2
    width = 256 if units % 256 == 0 else units
    chunks = units // width
    count = chunks * PIECES
    late = BF16 if rows <= 4 else F32
    wire = BF16 if cols <= 4 else F32
    vmem = pl.BlockSpec(memory_space=pltpu.VMEM)
    hbm = pl.BlockSpec(memory_space=pl.ANY)
    dma = pltpu.SemaphoreType.DMA
    *sums, tok_all, cot_all, res = pl.pallas_call(
        functools.partial(layer_kernel, rows, cols, depths),
        out_shape=(
            jax.ShapeDtypeStruct((2, block, feats), F32),
            *[jax.ShapeDtypeStruct((2, block, feats), late)] * (rows - 1),
            jax.ShapeDtypeStruct((total, feats), BF16),
            jax.ShapeDtypeStruct((total, feats), BF16),
            jax.ShapeDtypeStruct((chunks, 3, total, width), BF16),
        ),
        in_specs=[vmem, vmem, hbm, hbm, hbm],
        out_specs=(vmem,) * (rows + 3),
        scratch_shapes=[
            pltpu.VMEM((chunks, feats, width), BF16),
            pltpu.VMEM((chunks, feats, width), BF16),
            pltpu.VMEM((chunks, width, feats), BF16),
            pltpu.VMEM((chunks, 3, total, width), F32),
            pltpu.VMEM((2, count, 3, half // PIECES, width), wire),
            pltpu.VMEM((2, count, 3, half // PIECES, width), wire),
            pltpu.VMEM((2, total, feats), F32),
            pltpu.VMEM((depths - 1, rows, 2, block, feats), F32),
            dma((3, chunks)),
            dma((2, rows - 1)),
            dma((2, rows - 1)),
            dma((2, rows, depths - 1)),
            dma((2, rows, depths - 1)),
            dma((2, count, 2)),
            dma((2, count, 2)),
            dma((2, count)),
            dma((2, count)),
            dma((depths - 1, rows, 2)),
            dma((depths - 1, rows, 2)),
        ],
        compiler_params=pltpu.CompilerParams(
            collective_id=0, has_side_effects=True, vmem_limit_bytes=VMEM_BYTES
        ),
    )(tokens, cotangent, gate_weight, up_weight, down_weight)

    arrived = []
    for k in range(1, rows):
        ring = [(i, (i + k) % rows) for i in range(rows)]
        arrived.append(lax.ppermute(sums[k], "row", ring))
    out, tgrad = (
        sum((part[a].astype(F32) for part in arrived), sums[0][a]).astype(BF16) for a in range(2)
    )

    steps = max(n for n in (8, 4, 2, 1) if feats % (128 * n) == 0 and units % (16 * n) == 0)
    gate_grad, up_grad, down_grad = pl.pallas_call(
        functools.partial(grads_kernel, 1.0 / math.sqrt(total)),
        out_shape=(
            jax.ShapeDtypeStruct((feats, units), BF16),
            jax.ShapeDtypeStruct((feats, units), BF16),
            jax.ShapeDtypeStruct((units, feats), BF16),
        ),
        grid=(steps,),
        in_specs=[
            pl.BlockSpec((total, feats // steps), lambda i: (0, i)),
            pl.BlockSpec((total, feats), lambda i: (0, 0)),
            pl.BlockSpec((chunks, 3, total, width), lambda i: (0, 0, 0, 0)),
        ],
        out_specs=(
            pl.BlockSpec((feats // steps, units), lambda i: (i, 0)),
            pl.BlockSpec((feats // steps, units), lambda i: (i, 0)),
            pl.BlockSpec((units // steps, feats), lambda i: (i, 0)),
        ),
        scratch_shapes=[pltpu.VMEM((units, total), BF16)],
        cost_estimate=pl.CostEstimate(
            flops=6 * total * feats * units, bytes_accessed=6 * feats * units, transcendentals=0
        ),
        compiler_params=pltpu.CompilerParams(vmem_limit_bytes=GRADS_VMEM_BYTES),
    )(tok_all, cot_all, res)
    return (out, tgrad, gate_grad, up_grad, down_grad)


def solution(mesh):
    specs = (
        P(("row", "depth"), "col"),
        P(("row", "depth"), "col"),
        P("col", ("row", "depth")),
        P("col", ("row", "depth")),
        P(("row", "depth"), "col"),
    )
    sizes = (mesh.shape["row"], mesh.shape["col"], mesh.shape["depth"])
    return jax.shard_map(
        functools.partial(shards, *sizes), mesh=mesh, in_specs=specs, out_specs=specs, check_vma=False
    )
```

```python
import functools
import math

import jax
import jax.numpy as jnp
from jax import lax
from jax.experimental import pallas as pl
from jax.experimental.pallas import tpu as pltpu
from jax.sharding import PartitionSpec as P

F32 = jnp.float32
BF16 = jnp.bfloat16
MESH = pl.DeviceIdType.MESH
VMEM_BYTES = 58 * 1024 * 1024
EARLY = 3
HOP_STEPS = 3
PIECES = 2


def dot_nn(left, right):
    return lax.dot_general(left, right, (((1,), (0,)), ((), ())), preferred_element_type=F32)


def dot_nt(left, right):
    return lax.dot_general(left, right, (((1,), (1,)), ((), ())), preferred_element_type=F32)


def dot_tn(left, right):
    return lax.dot_general(left, right, (((0,), (0,)), ((), ())), preferred_element_type=F32)


def layer_kernel(
    rows, cols, depths,
    tok, cot, gw, uw, dw,
    *refs,
):
    sums, refs = refs[:rows], refs[rows:]
    tok_all, cot_all, res, gwv, uwv, dwv, part, sbuf, rbuf, acc, abuf, *refs = refs
    wsem, g1_send, g1_recv, g2_send, g2_recv, *refs = refs
    rs_send, rs_recv, ag_send, ag_recv, a_send, a_recv = refs
    chunks, _, width = gwv.shape
    block = tok.shape[0]
    total = tok_all.shape[0]
    half = total // 2
    piece = half // PIECES
    count = chunks * PIECES
    wire = sbuf.dtype
    r = lax.axis_index("row")
    z = lax.axis_index("col")
    d = lax.axis_index("depth")

    def rows_of(index):
        return pl.ds(pl.multiple_of(index * block, block), block)

    def weight_copy(c, i):
        span = slice(None) if chunks == 1 else pl.ds(pl.multiple_of(c * width, width), width)
        source = dw.at[span, :] if i == 2 else (gw, uw)[i].at[:, span]
        return pltpu.make_async_copy(source, (gwv, uwv, dwv)[i].at[c], wsem.at[i, c])

    def load(c):
        for i in range(3):
            weight_copy(c, i).start()

    early = min(EARLY, chunks)
    for c in range(early):
        load(c)

    barrier = pltpu.get_barrier_semaphore()
    for k in range(1, rows):
        pl.semaphore_signal(barrier, inc=1, device_id={"row": lax.rem(r + k, rows)}, device_id_type=MESH)
    for j in range(1, depths):
        pl.semaphore_signal(barrier, inc=1, device_id={"depth": lax.rem(d + j, depths)}, device_id_type=MESH)

    @pl.when(z > 0)
    def _():
        pl.semaphore_signal(barrier, inc=1, device_id={"col": z - 1}, device_id_type=MESH)

    @pl.when(z < cols - 1)
    def _():
        pl.semaphore_signal(barrier, inc=1, device_id={"col": z + 1}, device_id_type=MESH)

    for a, (mine, everyone) in enumerate(((tok, tok_all), (cot, cot_all))):
        everyone[rows_of(r * depths + d), :] = mine[...]
    acc[...] = jnp.zeros_like(acc)

    near = (rows - 1) + (depths - 1)

    @pl.when(jnp.logical_or(z == 0, z == cols - 1))
    def _():
        pl.semaphore_wait(barrier, near + 1)

    @pl.when(jnp.logical_and(z > 0, z < cols - 1))
    def _():
        pl.semaphore_wait(barrier, near + 2)

    pairs = ((tok, tok_all), (cot, cot_all))

    def first_hop(a, k, source_row):
        mine, everyone = pairs[a]
        return pltpu.make_async_remote_copy(
            src_ref=mine,
            dst_ref=everyone.at[rows_of(source_row * depths + d), :],
            send_sem=g1_send.at[a, k - 1],
            recv_sem=g1_recv.at[a, k - 1],
            device_id={"row": lax.rem(r + k, rows)},
            device_id_type=MESH,
        )

    def second_hop(a, k, j, source_depth):
        everyone = pairs[a][1]
        where = rows_of(lax.rem(r - k + rows, rows) * depths + source_depth)
        return pltpu.make_async_remote_copy(
            src_ref=everyone.at[where, :],
            dst_ref=everyone.at[where, :],
            send_sem=g2_send.at[a, k, j - 1],
            recv_sem=g2_recv.at[a, k, j - 1],
            device_id={"depth": lax.rem(d + j, depths)},
            device_id_type=MESH,
        )

    def gather(a):
        for k in range(rows):
            if k:
                first_hop(a, k, lax.rem(r - k + rows, rows)).wait_recv()
            for j in range(1, depths):
                second_hop(a, k, j, d).start()
        for k in range(rows):
            for j in range(1, depths):
                second_hop(a, k, j, lax.rem(d - j + depths, depths)).wait_recv()

    for a in range(2):
        for k in range(1, rows):
            first_hop(a, k, r).start()
    gather(0)

    def position(way):
        return z if way == 0 else cols - 1 - z

    def place(way, u):
        base = half if way == 0 else 0
        rows_at = pl.multiple_of(base + lax.rem(u, PIECES) * piece, piece)
        return lax.div(u, PIECES), pl.ds(rows_at, piece)

    spans = (pl.ds(0, 2), pl.ds(2, 1))

    def sum_copy(way, u, g):
        target = lax.rem(z + 1, cols) if way == 0 else lax.rem(z + cols - 1, cols)
        return pltpu.make_async_remote_copy(
            src_ref=sbuf.at[way, u, spans[g]],
            dst_ref=rbuf.at[way, u, spans[g]],
            send_sem=rs_send.at[way, u, g],
            recv_sem=rs_recv.at[way, u, g],
            device_id={"col": target},
            device_id_type=MESH,
        )

    def result_copy(way, u):
        target = lax.rem(z + cols - 1, cols) if way == 0 else lax.rem(z + 1, cols)
        c, mine = place(way, u)
        where = res.at[c, :, mine, :]
        return pltpu.make_async_remote_copy(
            src_ref=where,
            dst_ref=where,
            send_sem=ag_send.at[way, u],
            recv_sem=ag_recv.at[way, u],
            device_id={"col": target},
            device_id_type=MESH,
        )

    def gate_up_sums(c):
        @pl.when(c + early < chunks)
        def _():
            load(c + early)

        weight_copy(c, 0).wait()
        weight_copy(c, 1).wait()
        part[c, 0] = dot_nn(tok_all[...], gwv[c])
        part[c, 1] = dot_nn(tok_all[...], uwv[c])

    def cot_sums(c):
        weight_copy(c, 2).wait()
        part[c, 2] = dot_nt(cot_all[...], dwv[c])

    def pack(value):
        return (value * jnp.abs(value)).astype(wire) if wire == BF16 else value

    def unpack(value):
        if wire != BF16:
            return value
        value = value.astype(F32)
        root = jnp.sqrt(jnp.abs(value))
        return jnp.where(value < 0, -root, root)

    def first_sums(c, g):
        for way in range(2):

            @pl.when(position(way) == 0)
            def _():
                for h in range(PIECES):
                    u = c * PIECES + h
                    mine = place(way, u)[1]
                    sbuf[way, u, spans[g]] = pack(part[c, spans[g], mine, :])
                    sum_copy(way, u, g).start()

    def pass_sum(way, u):
        at = position(way)
        c, mine = place(way, u)
        for g in range(2):
            sum_copy(way, u, g).wait_recv()

        @pl.when(at < cols - 1)
        def _():
            sbuf[way, u] = pack(part[c, :, mine, :] + unpack(rbuf[way, u]))
            for g in range(2):
                sum_copy(way, u, g).start()

        @pl.when(at == cols - 1)
        def _():
            gate = part[c, 0, mine, :] + unpack(rbuf[way, u, 0])
            up = part[c, 1, mine, :] + unpack(rbuf[way, u, 1])
            hidden_cot = part[c, 2, mine, :] + unpack(rbuf[way, u, 2])
            sig = jax.nn.sigmoid(gate)
            res[c, 0, mine, :] = (gate * sig * up).astype(BF16)
            res[c, 1, mine, :] = (hidden_cot * up * sig * (1.0 + gate * (1.0 - sig))).astype(BF16)
            res[c, 2, mine, :] = (hidden_cot * gate * sig).astype(BF16)
            result_copy(way, u).start()

    def pass_result(way, u):
        result_copy(way, u).wait_recv()

        @pl.when(position(way) > 0)
        def _():
            result_copy(way, u).start()

    def depth_copy(a, row, j, target_depth):
        return pltpu.make_async_remote_copy(
            src_ref=acc.at[a, pl.ds(pl.multiple_of((row * depths + target_depth) * block, block), block), :],
            dst_ref=abuf.at[j - 1, row, a],
            send_sem=a_send.at[j - 1, row, a],
            recv_sem=a_recv.at[j - 1, row, a],
            device_id={"depth": lax.rem(d + j, depths)},
            device_id_type=MESH,
        )

    def send_output(a):
        for row in range(rows):
            for j in range(1, depths):
                depth_copy(a, row, j, lax.rem(d + j, depths)).start()

    def add_outputs(c):
        acc[0] += dot_nn(res[c, 0], dwv[c])

        @pl.when(c == chunks - 1)
        def _():
            send_output(0)

        acc[1] += dot_nt(res[c, 1], gwv[c]) + dot_nt(res[c, 2], uwv[c])

    last = cols - 1

    def within(u):
        return jnp.logical_and(u >= 0, u < count)

    def step(s, carry):
        for way in range(2):
            at = position(way)
            u = s - HOP_STEPS * at

            @pl.when(jnp.logical_and(at > 0, within(u)))
            def _():
                pass_sum(way, u)

        for way in range(2):
            at = position(way)
            u = s - HOP_STEPS * (last + last - at)

            @pl.when(jnp.logical_and(at < last, within(u)))
            def _():
                pass_result(way, u)

        @pl.when(jnp.logical_and(s < count, lax.rem(s, PIECES) == 0))
        def _():
            c = lax.div(s, PIECES)

            @pl.when(c >= early)
            def _():
                gate_up_sums(c)
                first_sums(c, 0)

            cot_sums(c)
            first_sums(c, 1)

        ready = s - HOP_STEPS * (last + jnp.maximum(z, last - z))

        @pl.when(jnp.logical_and(within(ready), lax.rem(ready + PIECES, PIECES) == PIECES - 1))
        def _():
            add_outputs(lax.div(ready, PIECES))

        return carry

    def head(c, carry):
        gate_up_sums(c)
        first_sums(c, 0)
        return carry

    lax.fori_loop(0, early, head, 0)
    gather(1)
    lax.fori_loop(0, count + HOP_STEPS * 2 * last, step, 0)

    send_output(1)
    for row in range(rows):
        for a in range(2):
            for j in range(1, depths):
                depth_copy(a, row, j, lax.rem(d + j, depths)).wait_recv()
    for k in range(rows):
        row = lax.rem(r + k, rows)
        for a in range(2):
            value = acc[a, rows_of(row * depths + d), :]
            for j in range(1, depths):
                value = value + abuf[j - 1, row, a]
            sums[k][a] = value.astype(sums[k].dtype)

    for k in range(1, rows):
        for a in range(2):
            first_hop(a, k, r).wait_send()
    for a in range(2):
        for k in range(rows):
            for j in range(1, depths):
                second_hop(a, k, j, d).wait_send()
                depth_copy(a, k, j, lax.rem(d + j, depths)).wait_send()

    def drain(u, carry):
        for way in range(2):
            at = position(way)

            @pl.when(at < cols - 1)
            def _():
                for g in range(2):
                    sum_copy(way, u, g).wait_send()

            @pl.when(at > 0)
            def _():
                result_copy(way, u).wait_send()

        return carry

    lax.fori_loop(0, count, drain, 0)


def grads_kernel(scale, tok, cot_all, res, gate_grad, up_grad, down_grad, hidden_t):
    chunks, _, _, width = res.shape
    i = pl.program_id(0)

    @pl.when(i == 0)
    def _():
        for c in range(chunks):
            hidden_t[pl.ds(c * width, width), :] = res[c, 0].T

    tok_t = tok[...].T
    for c in range(chunks):
        span = pl.ds(c * width, width)
        gate_grad[:, span] = (dot_nn(tok_t, res[c, 1]) * scale).astype(BF16)
        up_grad[:, span] = (dot_nn(tok_t, res[c, 2]) * scale).astype(BF16)
    size = down_grad.shape[0]
    mine = hidden_t[pl.ds(pl.multiple_of(i * size, size), size), :]
    down_grad[...] = (dot_nn(mine, cot_all[...]) * scale).astype(BF16)


def shards(rows, cols, depths, tokens, cotangent, gate_weight, up_weight, down_weight):
    block, feats = tokens.shape
    units = gate_weight.shape[1]
    total = block * rows * depths
    half = total // 2
    width = 256 if units % 256 == 0 else units
    chunks = units // width
    count = chunks * PIECES
    late = BF16 if rows <= 4 else F32
    wire = BF16 if cols <= 4 else F32
    vmem = pl.BlockSpec(memory_space=pltpu.VMEM)
    hbm = pl.BlockSpec(memory_space=pl.ANY)
    dma = pltpu.SemaphoreType.DMA
    *sums, tok_all, cot_all, res = pl.pallas_call(
        functools.partial(layer_kernel, rows, cols, depths),
        out_shape=(
            jax.ShapeDtypeStruct((2, block, feats), F32),
            *[jax.ShapeDtypeStruct((2, block, feats), late)] * (rows - 1),
            jax.ShapeDtypeStruct((total, feats), BF16),
            jax.ShapeDtypeStruct((total, feats), BF16),
            jax.ShapeDtypeStruct((chunks, 3, total, width), BF16),
        ),
        in_specs=[vmem, vmem, hbm, hbm, hbm],
        out_specs=(vmem,) * (rows + 3),
        scratch_shapes=[
            pltpu.VMEM((chunks, feats, width), BF16),
            pltpu.VMEM((chunks, feats, width), BF16),
            pltpu.VMEM((chunks, width, feats), BF16),
            pltpu.VMEM((chunks, 3, total, width), F32),
            pltpu.VMEM((2, count, 3, half // PIECES, width), wire),
            pltpu.VMEM((2, count, 3, half // PIECES, width), wire),
            pltpu.VMEM((2, total, feats), F32),
            pltpu.VMEM((depths - 1, rows, 2, block, feats), F32),
            dma((3, chunks)),
            dma((2, rows - 1)),
            dma((2, rows - 1)),
            dma((2, rows, depths - 1)),
            dma((2, rows, depths - 1)),
            dma((2, count, 2)),
            dma((2, count, 2)),
            dma((2, count)),
            dma((2, count)),
            dma((depths - 1, rows, 2)),
            dma((depths - 1, rows, 2)),
        ],
        compiler_params=pltpu.CompilerParams(
            collective_id=0, has_side_effects=True, vmem_limit_bytes=VMEM_BYTES
        ),
    )(tokens, cotangent, gate_weight, up_weight, down_weight)

    arrived = []
    for k in range(1, rows):
        ring = [(i, (i + k) % rows) for i in range(rows)]
        arrived.append(lax.ppermute(sums[k], "row", ring))
    out, tgrad = (
        sum((part[a].astype(F32) for part in arrived), sums[0][a]).astype(BF16) for a in range(2)
    )

    steps = max(n for n in (8, 4, 2, 1) if feats % (128 * n) == 0 and units % (16 * n) == 0)
    gate_grad, up_grad, down_grad = pl.pallas_call(
        functools.partial(grads_kernel, 1.0 / math.sqrt(total)),
        out_shape=(
            jax.ShapeDtypeStruct((feats, units), BF16),
            jax.ShapeDtypeStruct((feats, units), BF16),
            jax.ShapeDtypeStruct((units, feats), BF16),
        ),
        grid=(steps,),
        in_specs=[
            pl.BlockSpec((total, feats // steps), lambda i: (0, i)),
            pl.BlockSpec((total, feats), lambda i: (0, 0)),
            pl.BlockSpec((chunks, 3, total, width), lambda i: (0, 0, 0, 0)),
        ],
        out_specs=(
            pl.BlockSpec((feats // steps, units), lambda i: (i, 0)),
            pl.BlockSpec((feats // steps, units), lambda i: (i, 0)),
            pl.BlockSpec((units // steps, feats), lambda i: (i, 0)),
        ),
        scratch_shapes=[pltpu.VMEM((units, total), BF16)],
        cost_estimate=pl.CostEstimate(
            flops=6 * total * feats * units, bytes_accessed=6 * feats * units, transcendentals=0
        ),
        compiler_params=pltpu.CompilerParams(vmem_limit_bytes=VMEM_BYTES),
    )(tok_all, cot_all, res)
    return (out, tgrad, gate_grad, up_grad, down_grad)


def solution(mesh):
    specs = (
        P(("row", "depth"), "col"),
        P(("row", "depth"), "col"),
        P("col", ("row", "depth")),
        P("col", ("row", "depth")),
        P(("row", "depth"), "col"),
    )
    sizes = (mesh.shape["row"], mesh.shape["col"], mesh.shape["depth"])
    return jax.shard_map(
        functools.partial(shards, *sizes), mesh=mesh, in_specs=specs, out_specs=specs, check_vma=False
    )
```
